32 devices in a mesh: row: 8 (over z, y), col: 4 (over x, core).
Axes of the slice: x: 2, y: 2, z: 4, core: 2. Of those that a mesh axis runs over, the one named last changes fastest.
Arguments:
- train_points: float32 [16, 3, 8, 128], P(None, None, 'row'), may hold values from -6 to 6
- new_points: float32 [16, 256], replicated, may hold values from -6 to 6
- lengthscales: float32 [16], replicated, may hold values from 2.5 to 6
- factor: float32 [3, 8, 128, 3, 4, 256], P(None, 'row', None, None, 'col'), may hold values from -0.078125 to 0.078125
- diag_inverse: float32 [3, 8, 128, 4, 256], P(None, 'row', None, 'col'), may hold values from -3 to 3
Outputs:
- solution: float32 [3, 4, 8, 32, 256], P(None, 'col', 'row')
The draws below stay inside these ranges and needn't reach their ends.
All inputs are finite; a program needn't handle non-finite values.
Results may differ from the reference program's by a relative error of at most 0.0001.
Values sent between devices are 32-bit elements; how exact they have to be, the bound alone decides.
A program may use at most 128 MiB of HBM per device.

```python
import math
import jax
import jax.numpy as jnp
from jax import lax

DIMS = 16
NEW = 256
PANELS = 3
RB = 128
PW = 1024
QW = 256
QR = 32
TRAIN = 3072
N_ROW = 8
N_COL = 4


def draw_diag_inverse(key, part):
    first_key, second_key = jax.random.split(jax.random.fold_in(key, 7))
    shape = (PANELS, PW // RB, RB, PW // QW, QW)
    in_index = lax.broadcasted_iota(jnp.int32, shape, 1) * RB + lax.broadcasted_iota(jnp.int32, shape, 2)
    out_index = lax.broadcasted_iota(jnp.int32, shape, 3) * QW + lax.broadcasted_iota(jnp.int32, shape, 4)
    below = jnp.clip(jax.random.normal(first_key, shape, jnp.float32), -3.0, 3.0)
    middle = jax.random.uniform(second_key, shape, jnp.float32, 0.6, 1.6)
    below = below * (0.7 / math.sqrt(PW))
    values = jnp.where(out_index == in_index, middle, jnp.where(out_index > in_index, below, 0.0))
    return values.astype(jnp.float32)


def block_scale(rng, extent, shards, low, high):
    gain = 1.0
    for axis_at, blocks in shards:
        draws = jax.random.uniform(jax.random.fold_in(jax.random.fold_in(rng, 6), axis_at), (blocks,), jnp.float32, low / len(shards), high / len(shards))
        gain = gain * jnp.repeat(jnp.exp(draws), extent[axis_at] // blocks).reshape((-1,) + (1,) * (len(extent) - 1 - axis_at))
    return gain


def scatter_about(stream_key, shape, scale, most, cuts=(), held_as=jnp.bfloat16):
    result = jax.random.normal(stream_key, shape, jnp.float32) * scale
    if len(cuts) > 0:
        result = block_scale(stream_key, shape, cuts, -0.22, 0.18) * result
    return jnp.clip(result, min=-most, max=most).astype(held_as)


def setup_inputs(seed: int = 0) -> dict:
    key_of = jax.random.split(jax.random.key(seed), 6)
    return {
        "train_points": scatter_about(key_of[0], (DIMS, PANELS, N_ROW, RB), 1.0, 6.0, ((2, 8),), jnp.float32),
        "new_points": scatter_about(key_of[1], (DIMS, NEW), 1.0, 6.0, (), jnp.float32),
        "lengthscales": jnp.clip(jnp.exp(jax.random.uniform(key_of[2], (DIMS,), jnp.float32, math.log(2.5), math.log(6.0))), 2.5, 6.0),
        "factor": scatter_about(key_of[3], (PANELS, N_ROW, RB, PANELS, N_COL, QW), (2 * TRAIN) ** -0.5, 0.078125, ((1, 8), (4, 4)), jnp.float32),
        "diag_inverse": draw_diag_inverse(jax.random.fold_in(key_of[5], 71), 0),
    }


def reference(train_points, new_points, lengthscales, factor, diag_inverse):
    highest = lax.Precision.HIGHEST
    scaled_train = (train_points / lengthscales[:, None, None, None]).reshape(DIMS, TRAIN)
    scaled_new = new_points / lengthscales[:, None]
    inner_products = jnp.dot(scaled_train.T, scaled_new, precision=highest)
    sqdist = (jnp.sum(scaled_train * scaled_train, axis=0)[:, None]
              + jnp.sum(scaled_new * scaled_new, axis=0)[None, :] - 2.0 * inner_products)
    kernel = jnp.exp(-0.5 * sqdist)
    matrix = factor.reshape(TRAIN, TRAIN)
    inverses = diag_inverse.reshape(PANELS, PW, PW)
    pieces = []
    for panel in range(PANELS):
        first_row = panel * PW
        residual = kernel[first_row:first_row + PW]
        if panel > 0:
            solved_rows = jnp.concatenate(pieces, axis=0)
            residual = residual - jnp.dot(matrix[first_row:first_row + PW, :first_row], solved_rows, precision=highest)
        pieces.append(jnp.dot(inverses[panel].T, residual, precision=highest))
    solution = jnp.concatenate(pieces, axis=0)
    return solution.reshape(PANELS, N_COL, N_ROW, QR, NEW)
```

```python
import functools

import jax
import jax.numpy as jnp
from jax import lax
from jax.experimental import pallas as pl
from jax.experimental.pallas import tpu as pltpu
from jax.sharding import PartitionSpec as P

MESH = pl.DeviceIdType.MESH
HIGHEST = lax.Precision.HIGHEST
HALVES = 2


def dot(a, b):
    return jnp.dot(a, b, precision=HIGHEST, preferred_element_type=jnp.float32)


def blocks_below(panels):
    return [(k, j) for k in range(panels) for j in range(k)]


def kernel(
    n_row, n_col, panels, dims, unit,
    train_ref, new_ref, lens_ref, l_ref, w_ref, out_ref,
    train_peer, l_peer, w_cat, w_send, k_ref, r_buf, p_buf, p_in, x_buf, s_buf, s_in, acc,
    send_sem, recv_sem, pre_send, pre_recv,
):
    row, col = lax.axis_index("row"), lax.axis_index("col")
    n_s = n_row // 2
    s, t = row // 2, row % 2
    width = w_ref.shape[2]
    block_rows = w_ref.shape[1]
    mw = r_buf.shape[3]
    below = blocks_below(panels)
    pair = (2 * s + (1 - t), col)
    s_peers = [(d, (2 * ((s + d) % n_s) + t, col)) for d in range(1, n_s)]
    q_offsets = [(dt, dc) for dt in range(2) for dc in range(n_col) if dt + dc > 0]
    q_peers = [
        (dt, dc, (2 * s + (t + dt) % 2, (col + dc) % n_col)) for dt, dc in q_offsets
    ]

    barrier = pltpu.get_barrier_semaphore()
    for device in [p[-1] for p in s_peers] + [p[-1] for p in q_peers]:
        pl.semaphore_signal(barrier, inc=1, device_id=device, device_id_type=MESH)

    def rows(number):
        return pl.ds(pl.multiple_of(number * unit, unit), unit)

    def wait(ref, sem):
        pltpu.make_async_copy(ref, ref, sem).wait()

    def pair_copy(src, dst, number):
        return pltpu.make_async_remote_copy(
            src_ref=src, dst_ref=dst, send_sem=pre_send.at[number], recv_sem=pre_recv.at[number],
            device_id=pair, device_id_type=MESH,
        )

    copies = [pair_copy(train_ref, train_peer, 0)]
    for k in range(panels):
        copies.append(pair_copy(w_send.at[k], w_cat.at[k, :, pl.ds(block_rows, block_rows)], 1 + k))
    for b in range(len(below)):
        copies.append(pair_copy(l_ref.at[b], l_peer.at[b], 1 + panels + b))

    def split_inverse(k):
        for b in range(width // 128):
            turned = w_ref[k, :, b * 128:(b + 1) * 128].T
            even = [turned[i * unit:(i + 1) * unit] for i in range(0, 128 // unit, 2)]
            odd = [turned[i * unit:(i + 1) * unit] for i in range(1, 128 // unit, 2)]
            even, odd = jnp.concatenate(even, axis=0), jnp.concatenate(odd, axis=0)
            w_cat[k, b * 64:(b + 1) * 64, 0:block_rows] = jnp.where(t == 0, even, odd)
            w_send[k, b * 64:(b + 1) * 64, :] = jnp.where(t == 0, odd, even)

    split_inverse(0)
    pl.semaphore_wait(barrier, len(s_peers) + len(q_peers))
    copies[0].start()
    copies[1].start()
    for k in range(1, panels):
        split_inverse(k)
    order = []
    for b, (k, j) in enumerate(below):
        if j == 0:
            order.append(1 + k)
        order.append(1 + panels + b)
    for number in order:
        copies[number].start()

    diagonal = lax.broadcasted_iota(jnp.int32, (dims, dims), 0) == lax.broadcasted_iota(
        jnp.int32, (dims, dims), 1
    )
    lens = jnp.sum(
        jnp.where(diagonal, jnp.broadcast_to(lens_ref[...], (dims, dims)), 0.0), axis=1, keepdims=True
    )
    scaled_new = new_ref[...] / lens
    new_square = jnp.sum(scaled_new * scaled_new, axis=0, keepdims=True)

    def kernel_rows(points):
        turned = (points / lens).T
        square = jnp.sum(turned * turned, axis=1, keepdims=True)
        return jnp.exp(-0.5 * (square + new_square - 2.0 * dot(turned, scaled_new)))

    def panel_points(ref, k):
        return ref[pl.ds(k, dims, stride=panels), :]

    own = kernel_rows(panel_points(train_ref, 0))
    for h in range(HALVES):
        r_buf[0, h, 0:block_rows, :] = own[:, h * mw:(h + 1) * mw]
    for k in range(1, panels):
        k_ref[k] = kernel_rows(panel_points(train_ref, k))

    for k in range(panels - 1):
        for h in range(HALVES):
            for i in range(n_s):
                x_buf[k, h, rows(2 * i + 1 - t), :] = jnp.zeros((unit, mw), jnp.float32)

    copies[0].wait_recv()
    other = kernel_rows(panel_points(train_peer, 0))
    for h in range(HALVES):
        r_buf[0, h, block_rows:2 * block_rows, :] = other[:, h * mw:(h + 1) * mw]

    def sem_of(stage, k, h):
        return (stage * panels + k) * HALVES + h

    def send(stage, k, h, src, dst, device):
        number = sem_of(stage, k, h)
        pltpu.make_async_remote_copy(
            src_ref=src, dst_ref=dst, send_sem=send_sem.at[number], recv_sem=recv_sem.at[number],
            device_id=device, device_id_type=MESH,
        ).start()

    s_rows = pl.ds(0, len(s_peers) * unit)
    q_rows = pl.ds(0, len(q_peers) * unit)

    def apply_inverse(k, h):
        if k > 0:
            wait(r_buf.at[k, h, q_rows], recv_sem.at[sem_of(3, k - 1, h)])
        p_buf[k, h] = dot(w_cat[k], r_buf[k, h])
        for d, device in s_peers:
            send(0, k, h, p_buf.at[k, h, rows((s + d) % n_s)], p_in.at[k, h, rows(d - 1)], device)

    def sum_solved(k, h):
        wait(p_in.at[k, h, s_rows], recv_sem.at[sem_of(0, k, h)])
        total = p_buf[k, h, rows(s), :]
        for d in range(n_s - 1):
            total = total + p_in[k, h, d * unit:(d + 1) * unit, :]
        out_ref[k, :, h * mw:(h + 1) * mw] = total
        if k < panels - 1:
            x_buf[k, h, rows(row), :] = total
            for d, device in s_peers:
                send(1, k, h, x_buf.at[k, h, rows(row)], x_buf.at[k, h, rows(row)], device)

    def apply_factor(k, h):
        wait(x_buf.at[k, h, s_rows], recv_sem.at[sem_of(1, k, h)])
        x = x_buf[k, h]
        b = below.index((k + 1, k))
        for side, ref in enumerate((l_ref, l_peer)):
            change = dot(ref[b], x)
            part = pl.ds(side * block_rows, block_rows)
            s_buf[k, h, part, :] = change + acc[k + 1, h, part, :] if k > 0 else change
        for number, (dt, dc, device) in enumerate(q_peers):
            source = rows(dt * n_col + (col + dc) % n_col)
            send(2, k, h, s_buf.at[k, h, source], s_in.at[k, h, rows(number)], device)

    def look_ahead(k, h):
        x = x_buf[k, h]
        for later in range(k + 2, panels):
            b = below.index((later, k))
            for side, ref in enumerate((l_ref, l_peer)):
                change = dot(ref[b], x)
                part = pl.ds(side * block_rows, block_rows)
                acc[later, h, part, :] = change + acc[later, h, part, :] if k > 0 else change

    def sum_residual(k, h):
        wait(s_in.at[k, h, q_rows], recv_sem.at[sem_of(2, k, h)])
        total = s_buf[k, h, rows(col), :]
        for number in range(len(q_peers)):
            total = total + s_in[k, h, number * unit:(number + 1) * unit, :]
        r_buf[k + 1, h, rows(col), :] = k_ref[k + 1, rows(col), h * mw:(h + 1) * mw] - total
        for dt, dc, device in q_peers:
            send(
                3, k, h, r_buf.at[k + 1, h, rows(col)], r_buf.at[k + 1, h, rows(dt * n_col + col)], device
            )

    for k in range(panels):
        copies[1 + k].wait_recv()
        for h in range(HALVES):
            apply_inverse(k, h)
        for h in range(HALVES):
            sum_solved(k, h)
        if k < panels - 1:
            copies[1 + panels + below.index((k + 1, k))].wait_recv()
            for h in range(HALVES):
                apply_factor(k, h)
            for later in range(k + 2, panels):
                copies[1 + panels + below.index((later, k))].wait_recv()
            for h in range(HALVES):
                look_ahead(k, h)
            for h in range(HALVES):
                sum_residual(k, h)

    for copy in copies:
        copy.wait_send()
    for k in range(panels):
        for h in range(HALVES):
            wait(p_in.at[k, h, s_rows], send_sem.at[sem_of(0, k, h)])
            if k < panels - 1:
                wait(p_in.at[k, h, s_rows], send_sem.at[sem_of(1, k, h)])
                wait(s_in.at[k, h, q_rows], send_sem.at[sem_of(2, k, h)])
                wait(s_in.at[k, h, q_rows], send_sem.at[sem_of(3, k, h)])


def on_device(train_points, new_points, lengthscales, factor, diag_inverse):
    n_row, n_col = lax.axis_size("row"), lax.axis_size("col")
    panels, _, block_rows = factor.shape[:3]
    width = factor.shape[5]
    dims, new_count = new_points.shape
    unit = block_rows // n_col
    n_s = n_row // 2
    mw = new_count // HALVES
    below = blocks_below(panels)
    train = train_points.reshape(dims * panels, block_rows)
    lower = jnp.stack([factor[k, 0, :, j, 0, :] for k, j in below])
    inverse = diag_inverse.reshape(panels, block_rows, width)
    f32 = jnp.float32
    scratch = [
        pltpu.VMEM((dims * panels, block_rows), f32),
        pltpu.VMEM((len(below), block_rows, width), f32),
        pltpu.VMEM((panels, width // 2, 2 * block_rows), f32),
        pltpu.VMEM((panels, width // 2, block_rows), f32),
        pltpu.VMEM((panels, block_rows, new_count), f32),
        pltpu.VMEM((panels, HALVES, 2 * block_rows, mw), f32),
        pltpu.VMEM((panels, HALVES, width // 2, mw), f32),
        pltpu.VMEM((panels, HALVES, (n_s - 1) * unit, mw), f32),
        pltpu.VMEM((panels - 1, HALVES, width, mw), f32),
        pltpu.VMEM((panels - 1, HALVES, 2 * block_rows, mw), f32),
        pltpu.VMEM((panels - 1, HALVES, (2 * n_col - 1) * unit, mw), f32),
        pltpu.VMEM((panels, HALVES, 2 * block_rows, mw), f32),
        pltpu.SemaphoreType.DMA((4 * panels * HALVES,)),
        pltpu.SemaphoreType.DMA((4 * panels * HALVES,)),
        pltpu.SemaphoreType.DMA((1 + panels + len(below),)),
        pltpu.SemaphoreType.DMA((1 + panels + len(below),)),
    ]
    solved = pl.pallas_call(
        functools.partial(kernel, n_row, n_col, panels, dims, unit),
        out_shape=jax.ShapeDtypeStruct((panels, unit, new_count), f32),
        in_specs=[pl.BlockSpec(memory_space=pltpu.VMEM)] * 5,
        out_specs=pl.BlockSpec(memory_space=pltpu.VMEM),
        scratch_shapes=scratch,
        compiler_params=pltpu.CompilerParams(
            collective_id=0, has_side_effects=True,
            vmem_limit_bytes=(12 << 20) + 44 * block_rows * width * 4,
        ),
        cost_estimate=pl.CostEstimate(
            flops=12 * block_rows * width * new_count * panels,
            bytes_accessed=8 * panels * block_rows * width * 4,
            transcendentals=panels * block_rows * new_count,
        ),
    )(train, new_points, lengthscales.reshape(1, dims), lower, inverse)
    return solved.reshape(panels, 1, 1, unit, new_count)


def solution(mesh):
    return jax.shard_map(
        on_device,
        mesh=mesh,
        in_specs=(
            P(None, None, "row", None),
            P(),
            P(),
            P(None, "row", None, None, "col", None),
            P(None, "row", None, "col", None),
        ),
        out_specs=P(None, "col", "row", None, None),
        check_vma=False,
    )
```

```python
import functools

import jax
import jax.numpy as jnp
from jax import lax
from jax.experimental import pallas as pl
from jax.experimental.pallas import tpu as pltpu
from jax.sharding import PartitionSpec as P

MESH = pl.DeviceIdType.MESH
HIGHEST = lax.Precision.HIGHEST
HALVES = 2


def dot(a, b):
    return jnp.dot(a, b, precision=HIGHEST, preferred_element_type=jnp.float32)


def split(a):
    high = a.astype(jnp.bfloat16)
    return high, (a - high.astype(jnp.float32)).astype(jnp.bfloat16)


def dot_split(a_high, a_low, b):
    high, low = split(b)
    wide = jnp.dot(a_high, jnp.concatenate([high, low], axis=1), preferred_element_type=jnp.float32)
    cross = jnp.dot(a_low, high, preferred_element_type=jnp.float32)
    n = b.shape[1]
    return wide[:, :n] + (wide[:, n:] + cross)


def blocks_below(panels):
    return [(k, j) for k in range(panels) for j in range(k)]


def kernel(
    n_row, n_col, panels, dims, unit,
    train_ref, new_ref, lens_ref, l_ref, w_ref, out_ref,
    train_peer, l_peer, w_peer, w_send, w_high, w_low, l_high, l_low, k_ref, r_buf, p_buf, p_in, x_buf, s_buf, s_in, acc,
    send_sem, recv_sem, pre_send, pre_recv,
):
    row, col = lax.axis_index("row"), lax.axis_index("col")
    n_s = n_row // 2
    s, t = row // 2, row % 2
    width = w_ref.shape[2]
    block_rows = w_ref.shape[1]
    mw = r_buf.shape[3]
    below = blocks_below(panels)
    pair = (2 * s + (1 - t), col)
    s_peers = [(d, (2 * ((s + d) % n_s) + t, col)) for d in range(1, n_s)]
    q_offsets = [(dt, dc) for dt in range(2) for dc in range(n_col) if dt + dc > 0]
    q_peers = [
        (dt, dc, (2 * s + (t + dt) % 2, (col + dc) % n_col)) for dt, dc in q_offsets
    ]

    barrier = pltpu.get_barrier_semaphore()
    for device in [p[-1] for p in s_peers] + [p[-1] for p in q_peers]:
        pl.semaphore_signal(barrier, inc=1, device_id=device, device_id_type=MESH)

    def rows(number):
        return pl.ds(pl.multiple_of(number * unit, unit), unit)

    def wait(ref, sem):
        pltpu.make_async_copy(ref, ref, sem).wait()

    def pair_copy(src, dst, number):
        return pltpu.make_async_remote_copy(
            src_ref=src, dst_ref=dst, send_sem=pre_send.at[number], recv_sem=pre_recv.at[number],
            device_id=pair, device_id_type=MESH,
        )

    copies = [pair_copy(train_ref, train_peer, 0)]
    for k in range(panels):
        copies.append(pair_copy(w_send.at[k], w_peer.at[k], 1 + k))
    for b in range(len(below)):
        copies.append(pair_copy(l_ref.at[b], l_peer.at[b], 1 + panels + b))

    def split_inverse(k):
        for b in range(width // 128):
            turned = w_ref[k, :, b * 128:(b + 1) * 128].T
            even = [turned[i * unit:(i + 1) * unit] for i in range(0, 128 // unit, 2)]
            odd = [turned[i * unit:(i + 1) * unit] for i in range(1, 128 // unit, 2)]
            even, odd = jnp.concatenate(even, axis=0), jnp.concatenate(odd, axis=0)
            high, low = split(jnp.where(t == 0, even, odd))
            w_high[k, b * 64:(b + 1) * 64, 0:block_rows] = high
            w_low[k, b * 64:(b + 1) * 64, 0:block_rows] = low
            w_send[k, b * 64:(b + 1) * 64, :] = jnp.where(t == 0, odd, even)

    def keep_block(b, side, ref):
        high, low = split(ref[b])
        l_high[b, side * block_rows:(side + 1) * block_rows, :] = high
        l_low[b, side * block_rows:(side + 1) * block_rows, :] = low

    def take_block(b):
        copies[1 + panels + b].wait_recv()
        keep_block(b, 1, l_peer)

    def take_inverse(k):
        copies[1 + k].wait_recv()
        high, low = split(w_peer[k])
        w_high[k, :, block_rows:2 * block_rows] = high
        w_low[k, :, block_rows:2 * block_rows] = low

    split_inverse(0)
    diagonal = lax.broadcasted_iota(jnp.int32, (dims, dims), 0) == lax.broadcasted_iota(
        jnp.int32, (dims, dims), 1
    )
    lens = jnp.sum(
        jnp.where(diagonal, jnp.broadcast_to(lens_ref[...], (dims, dims)), 0.0), axis=1, keepdims=True
    )
    scaled_new = new_ref[...] / lens
    new_square = jnp.sum(scaled_new * scaled_new, axis=0, keepdims=True)

    def kernel_rows(points):
        turned = (points / lens).T
        square = jnp.sum(turned * turned, axis=1, keepdims=True)
        return jnp.exp(-0.5 * (square + new_square - 2.0 * dot(turned, scaled_new)))

    def panel_points(ref, k):
        return ref[pl.ds(k, dims, stride=panels), :]

    own = kernel_rows(panel_points(train_ref, 0))
    for h in range(HALVES):
        r_buf[0, h, 0:block_rows, :] = own[:, h * mw:(h + 1) * mw]
    pl.semaphore_wait(barrier, len(s_peers) + len(q_peers))
    copies[0].start()
    copies[1].start()
    for k in range(1, panels):
        split_inverse(k)
    order = []
    for b, (k, j) in enumerate(below):
        if j == 0:
            order.append(1 + k)
        order.append(1 + panels + b)
    for number in order:
        copies[number].start()

    for k in range(1, panels):
        k_ref[k] = kernel_rows(panel_points(train_ref, k))

    for k in range(panels - 1):
        for h in range(HALVES):
            for i in range(n_s):
                x_buf[k, h, rows(2 * i + 1 - t), :] = jnp.zeros((unit, mw), jnp.float32)

    for b in range(len(below)):
        keep_block(b, 0, l_ref)

    copies[0].wait_recv()
    other = kernel_rows(panel_points(train_peer, 0))
    for h in range(HALVES):
        r_buf[0, h, block_rows:2 * block_rows, :] = other[:, h * mw:(h + 1) * mw]

    def sem_of(stage, k, h):
        return (stage * panels + k) * HALVES + h

    def send(stage, k, h, src, dst, device):
        number = sem_of(stage, k, h)
        pltpu.make_async_remote_copy(
            src_ref=src, dst_ref=dst, send_sem=send_sem.at[number], recv_sem=recv_sem.at[number],
            device_id=device, device_id_type=MESH,
        ).start()

    s_rows = pl.ds(0, len(s_peers) * unit)
    q_rows = pl.ds(0, len(q_peers) * unit)

    def apply_inverse(k, h):
        if k > 0:
            wait(r_buf.at[k, h, q_rows], recv_sem.at[sem_of(3, k - 1, h)])
        p_buf[k, h] = dot_split(w_high[k], w_low[k], r_buf[k, h])
        for d, device in s_peers:
            send(0, k, h, p_buf.at[k, h, rows((s + d) % n_s)], p_in.at[k, h, rows(d - 1)], device)

    def sum_solved(k, h):
        wait(p_in.at[k, h, s_rows], recv_sem.at[sem_of(0, k, h)])
        total = p_buf[k, h, rows(s), :]
        for d in range(n_s - 1):
            total = total + p_in[k, h, d * unit:(d + 1) * unit, :]
        out_ref[k, :, h * mw:(h + 1) * mw] = total
        if k < panels - 1:
            x_buf[k, h, rows(row), :] = total
            for d, device in s_peers:
                send(1, k, h, x_buf.at[k, h, rows(row)], x_buf.at[k, h, rows(row)], device)

    def apply_factor(k, h):
        wait(x_buf.at[k, h, s_rows], recv_sem.at[sem_of(1, k, h)])
        x = x_buf[k, h]
        b = below.index((k + 1, k))
        change = dot_split(l_high[b], l_low[b], x)
        s_buf[k, h] = change + acc[k + 1, h] if k > 0 else change
        for number, (dt, dc, device) in enumerate(q_peers):
            source = rows(dt * n_col + (col + dc) % n_col)
            send(2, k, h, s_buf.at[k, h, source], s_in.at[k, h, rows(number)], device)

    def look_ahead(k, h):
        x = x_buf[k, h]
        for later in range(k + 2, panels):
            b = below.index((later, k))
            change = dot_split(l_high[b], l_low[b], x)
            acc[later, h] = change + acc[later, h] if k > 0 else change

    def sum_residual(k, h):
        wait(s_in.at[k, h, q_rows], recv_sem.at[sem_of(2, k, h)])
        total = s_buf[k, h, rows(col), :]
        for number in range(len(q_peers)):
            total = total + s_in[k, h, number * unit:(number + 1) * unit, :]
        r_buf[k + 1, h, rows(col), :] = k_ref[k + 1, rows(col), h * mw:(h + 1) * mw] - total
        for dt, dc, device in q_peers:
            send(
                3, k, h, r_buf.at[k + 1, h, rows(col)], r_buf.at[k + 1, h, rows(dt * n_col + col)], device
            )

    take_inverse(0)
    for k in range(panels):
        for h in range(HALVES):
            apply_inverse(k, h)
        if k < panels - 1:
            take_block(below.index((k + 1, k)))
        for h in range(HALVES):
            sum_solved(k, h)
        if k < panels - 1:
            for h in range(HALVES):
                apply_factor(k, h)
            take_inverse(k + 1)
            for later in range(k + 2, panels):
                take_block(below.index((later, k)))
            for h in range(HALVES):
                look_ahead(k, h)
            for h in range(HALVES):
                sum_residual(k, h)

    for copy in copies:
        copy.wait_send()
    for k in range(panels):
        for h in range(HALVES):
            wait(p_in.at[k, h, s_rows], send_sem.at[sem_of(0, k, h)])
            if k < panels - 1:
                wait(p_in.at[k, h, s_rows], send_sem.at[sem_of(1, k, h)])
                wait(s_in.at[k, h, q_rows], send_sem.at[sem_of(2, k, h)])
                wait(s_in.at[k, h, q_rows], send_sem.at[sem_of(3, k, h)])


def on_device(train_points, new_points, lengthscales, factor, diag_inverse):
    n_row, n_col = lax.axis_size("row"), lax.axis_size("col")
    panels, _, block_rows = factor.shape[:3]
    width = factor.shape[5]
    dims, new_count = new_points.shape
    unit = block_rows // n_col
    n_s = n_row // 2
    mw = new_count // HALVES
    below = blocks_below(panels)
    train = train_points.reshape(dims * panels, block_rows)
    lower = jnp.stack([factor[k, 0, :, j, 0, :] for k, j in below])
    inverse = diag_inverse.reshape(panels, block_rows, width)
    f32 = jnp.float32
    scratch = [
        pltpu.VMEM((dims * panels, block_rows), f32),
        pltpu.VMEM((len(below), block_rows, width), f32),
        pltpu.VMEM((panels, width // 2, block_rows), f32),
        pltpu.VMEM((panels, width // 2, block_rows), f32),
        pltpu.VMEM((panels, width // 2, 2 * block_rows), jnp.bfloat16),
        pltpu.VMEM((panels, width // 2, 2 * block_rows), jnp.bfloat16),
        pltpu.VMEM((len(below), 2 * block_rows, width), jnp.bfloat16),
        pltpu.VMEM((len(below), 2 * block_rows, width), jnp.bfloat16),
        pltpu.VMEM((panels, block_rows, new_count), f32),
        pltpu.VMEM((panels, HALVES, 2 * block_rows, mw), f32),
        pltpu.VMEM((panels, HALVES, width // 2, mw), f32),
        pltpu.VMEM((panels, HALVES, (n_s - 1) * unit, mw), f32),
        pltpu.VMEM((panels - 1, HALVES, width, mw), f32),
        pltpu.VMEM((panels - 1, HALVES, 2 * block_rows, mw), f32),
        pltpu.VMEM((panels - 1, HALVES, (2 * n_col - 1) * unit, mw), f32),
        pltpu.VMEM((panels, HALVES, 2 * block_rows, mw), f32),
        pltpu.SemaphoreType.DMA((4 * panels * HALVES,)),
        pltpu.SemaphoreType.DMA((4 * panels * HALVES,)),
        pltpu.SemaphoreType.DMA((1 + panels + len(below),)),
        pltpu.SemaphoreType.DMA((1 + panels + len(below),)),
    ]
    solved = pl.pallas_call(
        functools.partial(kernel, n_row, n_col, panels, dims, unit),
        out_shape=jax.ShapeDtypeStruct((panels, unit, new_count), f32),
        in_specs=[pl.BlockSpec(memory_space=pltpu.VMEM)] * 5,
        out_specs=pl.BlockSpec(memory_space=pltpu.VMEM),
        scratch_shapes=scratch,
        compiler_params=pltpu.CompilerParams(
            collective_id=0, has_side_effects=True,
            vmem_limit_bytes=(12 << 20) + 44 * block_rows * width * 4,
        ),
        cost_estimate=pl.CostEstimate(
            flops=12 * block_rows * width * new_count * panels,
            bytes_accessed=8 * panels * block_rows * width * 4,
            transcendentals=panels * block_rows * new_count,
        ),
    )(train, new_points, lengthscales.reshape(1, dims), lower, inverse)
    return solved.reshape(panels, 1, 1, unit, new_count)


def solution(mesh):
    return jax.shard_map(
        on_device,
        mesh=mesh,
        in_specs=(
            P(None, None, "row", None),
            P(),
            P(),
            P(None, "row", None, None, "col", None),
            P(None, "row", None, "col", None),
        ),
        out_specs=P(None, "col", "row", None, None),
        check_vma=False,
    )
```

```python
import functools

import jax
import jax.numpy as jnp
from jax import lax
from jax.experimental import pallas as pl
from jax.experimental.pallas import tpu as pltpu
from jax.sharding import PartitionSpec as P

MESH = pl.DeviceIdType.MESH
HIGHEST = lax.Precision.HIGHEST
HALVES = 2


def dot(a, b):
    return jnp.dot(a, b, precision=HIGHEST, preferred_element_type=jnp.float32)


def split(a):
    high = a.astype(jnp.bfloat16)
    return high, (a - high.astype(jnp.float32)).astype(jnp.bfloat16)


def dot_split(a_high, a_low, b):
    high, low = split(b)
    wide = jnp.dot(a_high, jnp.concatenate([high, low], axis=1), preferred_element_type=jnp.float32)
    cross = jnp.dot(a_low, high, preferred_element_type=jnp.float32)
    n = b.shape[1]
    return wide[:, :n] + (wide[:, n:] + cross)


def blocks_below(panels):
    return [(k, j) for k in range(panels) for j in range(k)]


def kernel(
    n_row, n_col, panels, dims, unit,
    train_ref, new_ref, lens_ref, l_ref, w_ref, out_ref,
    train_peer, l_peer, w_peer, w_send, w_high, w_low, l_high, l_low, k_ref, r_buf, p_buf, p_in, x_buf, s_buf, s_in, acc,
    send_sem, recv_sem, pre_send, pre_recv,
):
    row, col = lax.axis_index("row"), lax.axis_index("col")
    n_s = n_row // 2
    s, t = row // 2, row % 2
    width = w_ref.shape[2]
    block_rows = w_ref.shape[1]
    mw = r_buf.shape[3]
    below = blocks_below(panels)
    pair = (2 * s + (1 - t), col)
    s_peers = [(d, (2 * ((s + d) % n_s) + t, col)) for d in range(1, n_s)]
    q_offsets = [(dt, dc) for dt in range(2) for dc in range(n_col) if dt + dc > 0]
    q_peers = [
        (dt, dc, (2 * s + (t + dt) % 2, (col + dc) % n_col)) for dt, dc in q_offsets
    ]

    barrier = pltpu.get_barrier_semaphore()
    for device in [p[-1] for p in s_peers] + [p[-1] for p in q_peers]:
        pl.semaphore_signal(barrier, inc=1, device_id=device, device_id_type=MESH)

    def rows(number):
        return pl.ds(pl.multiple_of(number * unit, unit), unit)

    def wait(ref, sem):
        pltpu.make_async_copy(ref, ref, sem).wait()

    def pair_copy(src, dst, number):
        return pltpu.make_async_remote_copy(
            src_ref=src, dst_ref=dst, send_sem=pre_send.at[number], recv_sem=pre_recv.at[number],
            device_id=pair, device_id_type=MESH,
        )

    copies = [pair_copy(train_ref, train_peer, 0)]
    for k in range(panels):
        copies.append(pair_copy(w_send.at[k], w_peer.at[k], 1 + k))
    for b in range(len(below)):
        copies.append(pair_copy(l_ref.at[b], l_peer.at[b], 1 + panels + b))

    def split_inverse(k):
        for b in range(width // 128):
            turned = w_ref[k, :, b * 128:(b + 1) * 128].T
            even = [turned[i * unit:(i + 1) * unit] for i in range(0, 128 // unit, 2)]
            odd = [turned[i * unit:(i + 1) * unit] for i in range(1, 128 // unit, 2)]
            even, odd = jnp.concatenate(even, axis=0), jnp.concatenate(odd, axis=0)
            high, low = split(jnp.where(t == 0, even, odd))
            w_high[k, b * 64:(b + 1) * 64, 0:block_rows] = high
            w_low[k, b * 64:(b + 1) * 64, 0:block_rows] = low
            w_send[k, b * 64:(b + 1) * 64, :] = jnp.where(t == 0, odd, even)

    def keep_block(b, side, ref):
        high, low = split(ref[b])
        l_high[b, side * block_rows:(side + 1) * block_rows, :] = high
        l_low[b, side * block_rows:(side + 1) * block_rows, :] = low

    def take_block(b):
        copies[1 + panels + b].wait_recv()
        keep_block(b, 1, l_peer)

    def take_inverse(k):
        copies[1 + k].wait_recv()
        high, low = split(w_peer[k])
        w_high[k, :, block_rows:2 * block_rows] = high
        w_low[k, :, block_rows:2 * block_rows] = low

    split_inverse(0)
    diagonal = lax.broadcasted_iota(jnp.int32, (dims, dims), 0) == lax.broadcasted_iota(
        jnp.int32, (dims, dims), 1
    )
    lens = jnp.sum(
        jnp.where(diagonal, jnp.broadcast_to(lens_ref[...], (dims, dims)), 0.0), axis=1, keepdims=True
    )
    scaled_new = new_ref[...] / lens
    new_square = jnp.sum(scaled_new * scaled_new, axis=0, keepdims=True)

    def kernel_rows(points):
        turned = (points / lens).T
        square = jnp.sum(turned * turned, axis=1, keepdims=True)
        return jnp.exp(-0.5 * (square + new_square - 2.0 * dot(turned, scaled_new)))

    def panel_points(ref, k):
        return ref[pl.ds(k, dims, stride=panels), :]

    own = kernel_rows(panel_points(train_ref, 0))
    for h in range(HALVES):
        r_buf[0, h, 0:block_rows, :] = own[:, h * mw:(h + 1) * mw]
    pl.semaphore_wait(barrier, len(s_peers) + len(q_peers))
    copies[0].start()
    copies[1].start()
    for k in range(1, panels):
        split_inverse(k)
    for k in range(1, panels):
        k_ref[k] = kernel_rows(panel_points(train_ref, k))

    for k in range(panels - 1):
        for h in range(HALVES):
            for i in range(n_s):
                x_buf[k, h, rows(2 * i + 1 - t), :] = jnp.zeros((unit, mw), jnp.float32)

    for b in range(len(below)):
        keep_block(b, 0, l_ref)

    copies[0].wait_recv()
    other = kernel_rows(panel_points(train_peer, 0))
    for h in range(HALVES):
        r_buf[0, h, block_rows:2 * block_rows, :] = other[:, h * mw:(h + 1) * mw]

    def sem_of(stage, k, h):
        return (stage * panels + k) * HALVES + h

    def send(stage, k, h, src, dst, device):
        number = sem_of(stage, k, h)
        pltpu.make_async_remote_copy(
            src_ref=src, dst_ref=dst, send_sem=send_sem.at[number], recv_sem=recv_sem.at[number],
            device_id=device, device_id_type=MESH,
        ).start()

    s_rows = pl.ds(0, len(s_peers) * unit)
    q_rows = pl.ds(0, len(q_peers) * unit)

    def apply_inverse(k, h):
        if k > 0:
            wait(r_buf.at[k, h, q_rows], recv_sem.at[sem_of(3, k - 1, h)])
        p_buf[k, h] = dot_split(w_high[k], w_low[k], r_buf[k, h])
        for d, device in s_peers:
            send(0, k, h, p_buf.at[k, h, rows((s + d) % n_s)], p_in.at[k, h, rows(d - 1)], device)

    def sum_solved(k, h):
        wait(p_in.at[k, h, s_rows], recv_sem.at[sem_of(0, k, h)])
        total = p_buf[k, h, rows(s), :]
        for d in range(n_s - 1):
            total = total + p_in[k, h, d * unit:(d + 1) * unit, :]
        out_ref[k, :, h * mw:(h + 1) * mw] = total
        if k < panels - 1:
            x_buf[k, h, rows(row), :] = total
            for d, device in s_peers:
                send(1, k, h, x_buf.at[k, h, rows(row)], x_buf.at[k, h, rows(row)], device)

    def apply_factor(k, h):
        wait(x_buf.at[k, h, s_rows], recv_sem.at[sem_of(1, k, h)])
        x = x_buf[k, h]
        b = below.index((k + 1, k))
        change = dot_split(l_high[b], l_low[b], x)
        s_buf[k, h] = change + acc[k + 1, h] if k > 0 else change
        for number, (dt, dc, device) in enumerate(q_peers):
            source = rows(dt * n_col + (col + dc) % n_col)
            send(2, k, h, s_buf.at[k, h, source], s_in.at[k, h, rows(number)], device)

    def add_earlier(k, j, h):
        b = below.index((k + 1, j))
        change = dot_split(l_high[b], l_low[b], x_buf[j, h])
        acc[k + 1, h] = change + acc[k + 1, h] if j > 0 else change

    def sum_residual(k, h):
        wait(s_in.at[k, h, q_rows], recv_sem.at[sem_of(2, k, h)])
        total = s_buf[k, h, rows(col), :]
        for number in range(len(q_peers)):
            total = total + s_in[k, h, number * unit:(number + 1) * unit, :]
        r_buf[k + 1, h, rows(col), :] = k_ref[k + 1, rows(col), h * mw:(h + 1) * mw] - total
        for dt, dc, device in q_peers:
            send(
                3, k, h, r_buf.at[k + 1, h, rows(col)], r_buf.at[k + 1, h, rows(dt * n_col + col)], device
            )

    take_inverse(0)
    for k in range(panels):
        for h in range(HALVES):
            apply_inverse(k, h)
        if k < panels - 1:
            for j in range(k, -1, -1):
                copies[1 + panels + below.index((k + 1, j))].start()
        for h in range(HALVES):
            sum_solved(k, h)
        if k < panels - 1:
            copies[1 + k + 1].start()
            for j in range(k, -1, -1):
                take_block(below.index((k + 1, j)))
            for j in range(k):
                for h in range(HALVES):
                    add_earlier(k, j, h)
        if k < panels - 1:
            for h in range(HALVES):
                apply_factor(k, h)
            take_inverse(k + 1)
            for h in range(HALVES):
                sum_residual(k, h)

    for copy in copies:
        copy.wait_send()
    for k in range(panels):
        for h in range(HALVES):
            wait(p_in.at[k, h, s_rows], send_sem.at[sem_of(0, k, h)])
            if k < panels - 1:
                wait(p_in.at[k, h, s_rows], send_sem.at[sem_of(1, k, h)])
                wait(s_in.at[k, h, q_rows], send_sem.at[sem_of(2, k, h)])
                wait(s_in.at[k, h, q_rows], send_sem.at[sem_of(3, k, h)])


def on_device(train_points, new_points, lengthscales, factor, diag_inverse):
    n_row, n_col = lax.axis_size("row"), lax.axis_size("col")
    panels, _, block_rows = factor.shape[:3]
    width = factor.shape[5]
    dims, new_count = new_points.shape
    unit = block_rows // n_col
    n_s = n_row // 2
    mw = new_count // HALVES
    below = blocks_below(panels)
    train = train_points.reshape(dims * panels, block_rows)
    lower = jnp.stack([factor[k, 0, :, j, 0, :] for k, j in below])
    inverse = diag_inverse.reshape(panels, block_rows, width)
    f32 = jnp.float32
    scratch = [
        pltpu.VMEM((dims * panels, block_rows), f32),
        pltpu.VMEM((len(below), block_rows, width), f32),
        pltpu.VMEM((panels, width // 2, block_rows), f32),
        pltpu.VMEM((panels, width // 2, block_rows), f32),
        pltpu.VMEM((panels, width // 2, 2 * block_rows), jnp.bfloat16),
        pltpu.VMEM((panels, width // 2, 2 * block_rows), jnp.bfloat16),
        pltpu.VMEM((len(below), 2 * block_rows, width), jnp.bfloat16),
        pltpu.VMEM((len(below), 2 * block_rows, width), jnp.bfloat16),
        pltpu.VMEM((panels, block_rows, new_count), f32),
        pltpu.VMEM((panels, HALVES, 2 * block_rows, mw), f32),
        pltpu.VMEM((panels, HALVES, width // 2, mw), f32),
        pltpu.VMEM((panels, HALVES, (n_s - 1) * unit, mw), f32),
        pltpu.VMEM((panels - 1, HALVES, width, mw), f32),
        pltpu.VMEM((panels - 1, HALVES, 2 * block_rows, mw), f32),
        pltpu.VMEM((panels - 1, HALVES, (2 * n_col - 1) * unit, mw), f32),
        pltpu.VMEM((panels, HALVES, 2 * block_rows, mw), f32),
        pltpu.SemaphoreType.DMA((4 * panels * HALVES,)),
        pltpu.SemaphoreType.DMA((4 * panels * HALVES,)),
        pltpu.SemaphoreType.DMA((1 + panels + len(below),)),
        pltpu.SemaphoreType.DMA((1 + panels + len(below),)),
    ]
    solved = pl.pallas_call(
        functools.partial(kernel, n_row, n_col, panels, dims, unit),
        out_shape=jax.ShapeDtypeStruct((panels, unit, new_count), f32),
        in_specs=[pl.BlockSpec(memory_space=pltpu.VMEM)] * 5,
        out_specs=pl.BlockSpec(memory_space=pltpu.VMEM),
        scratch_shapes=scratch,
        compiler_params=pltpu.CompilerParams(
            collective_id=0, has_side_effects=True,
            vmem_limit_bytes=(12 << 20) + 44 * block_rows * width * 4,
        ),
        cost_estimate=pl.CostEstimate(
            flops=12 * block_rows * width * new_count * panels,
            bytes_accessed=8 * panels * block_rows * width * 4,
            transcendentals=panels * block_rows * new_count,
        ),
    )(train, new_points, lengthscales.reshape(1, dims), lower, inverse)
    return solved.reshape(panels, 1, 1, unit, new_count)


def solution(mesh):
    return jax.shard_map(
        on_device,
        mesh=mesh,
        in_specs=(
            P(None, None, "row", None),
            P(),
            P(),
            P(None, "row", None, None, "col", None),
            P(None, "row", None, "col", None),
        ),
        out_specs=P(None, "col", "row", None, None),
        check_vma=False,
    )
```

```python
import functools

import jax
import jax.numpy as jnp
from jax import lax
from jax.experimental import pallas as pl
from jax.experimental.pallas import tpu as pltpu
from jax.sharding import PartitionSpec as P

MESH = pl.DeviceIdType.MESH
HIGHEST = lax.Precision.HIGHEST
HALVES = 2
LAG = 2


def dot(a, b):
    return jnp.dot(a, b, precision=HIGHEST, preferred_element_type=jnp.float32)


def split(a):
    high = a.astype(jnp.bfloat16)
    return high, (a - high.astype(jnp.float32)).astype(jnp.bfloat16)


def dot_split(a_high, a_low, b):
    high, low = split(b)
    wide = jnp.dot(a_high, jnp.concatenate([high, low], axis=1), preferred_element_type=jnp.float32)
    cross = jnp.dot(a_low, high, preferred_element_type=jnp.float32)
    n = b.shape[1]
    return wide[:, :n] + (wide[:, n:] + cross)


def blocks_below(panels):
    return [(k, j) for k in range(panels) for j in range(k)]


def kernel(
    n_row, n_col, panels, dims, unit,
    train_ref, new_ref, lens_ref, l_ref, w_ref, out_ref,
    train_peer, l_peer, w_peer, w_send, w_high, w_low, l_high, l_low, k_ref, r_buf, p_buf, p_in, x_buf, s_buf, s_in, acc,
    send_sem, recv_sem, pre_send, pre_recv,
):
    row, col = lax.axis_index("row"), lax.axis_index("col")
    n_s = n_row // 2
    s, t = row // 2, row % 2
    width = w_ref.shape[2]
    block_rows = w_ref.shape[1]
    mw = r_buf.shape[3]
    below = blocks_below(panels)
    pair = (2 * s + (1 - t), col)
    s_peers = [(d, (2 * ((s + d) % n_s) + t, col)) for d in range(1, n_s)]
    q_offsets = [(dt, dc) for dt in range(2) for dc in range(n_col) if dt + dc > 0]
    q_peers = [
        (dt, dc, (2 * s + (t + dt) % 2, (col + dc) % n_col)) for dt, dc in q_offsets
    ]

    barrier = pltpu.get_barrier_semaphore()
    for device in [p[-1] for p in s_peers] + [p[-1] for p in q_peers]:
        pl.semaphore_signal(barrier, inc=1, device_id=device, device_id_type=MESH)

    def rows(number):
        return pl.ds(pl.multiple_of(number * unit, unit), unit)

    def wait(ref, sem):
        pltpu.make_async_copy(ref, ref, sem).wait()

    def pair_copy(src, dst, number):
        return pltpu.make_async_remote_copy(
            src_ref=src, dst_ref=dst, send_sem=pre_send.at[number], recv_sem=pre_recv.at[number],
            device_id=pair, device_id_type=MESH,
        )

    copies = [pair_copy(train_ref, train_peer, 0)]
    for k in range(panels):
        copies.append(pair_copy(w_send.at[k], w_peer.at[k], 1 + k))
    for b in range(len(below)):
        copies.append(pair_copy(l_ref.at[b], l_peer.at[b], 1 + panels + b))

    def split_inverse(k):
        for b in range(width // 128):
            turned = w_ref[k, :, b * 128:(b + 1) * 128].T
            even = [turned[i * unit:(i + 1) * unit] for i in range(0, 128 // unit, 2)]
            odd = [turned[i * unit:(i + 1) * unit] for i in range(1, 128 // unit, 2)]
            even, odd = jnp.concatenate(even, axis=0), jnp.concatenate(odd, axis=0)
            high, low = split(jnp.where(t == 0, even, odd))
            w_high[k, b * 64:(b + 1) * 64, 0:block_rows] = high
            w_low[k, b * 64:(b + 1) * 64, 0:block_rows] = low
            w_send[k, b * 64:(b + 1) * 64, :] = jnp.where(t == 0, odd, even)

    def keep_block(b, side, ref):
        high, low = split(ref[b])
        l_high[b, side * block_rows:(side + 1) * block_rows, :] = high
        l_low[b, side * block_rows:(side + 1) * block_rows, :] = low

    def take_block(b):
        copies[1 + panels + b].wait_recv()
        keep_block(b, 1, l_peer)

    def take_inverse(k):
        copies[1 + k].wait_recv()
        high, low = split(w_peer[k])
        w_high[k, :, block_rows:2 * block_rows] = high
        w_low[k, :, block_rows:2 * block_rows] = low

    split_inverse(0)
    diagonal = lax.broadcasted_iota(jnp.int32, (dims, dims), 0) == lax.broadcasted_iota(
        jnp.int32, (dims, dims), 1
    )
    lens = jnp.sum(
        jnp.where(diagonal, jnp.broadcast_to(lens_ref[...], (dims, dims)), 0.0), axis=1, keepdims=True
    )
    scaled_new = new_ref[...] / lens
    new_square = jnp.sum(scaled_new * scaled_new, axis=0, keepdims=True)

    def kernel_rows(points):
        turned = (points / lens).T
        square = jnp.sum(turned * turned, axis=1, keepdims=True)
        return jnp.exp(-0.5 * (square + new_square - 2.0 * dot(turned, scaled_new)))

    def panel_points(ref, k):
        return ref[pl.ds(k, dims, stride=panels), :]

    own = kernel_rows(panel_points(train_ref, 0))
    for h in range(HALVES):
        r_buf[0, h, 0:block_rows, :] = own[:, h * mw:(h + 1) * mw]
    pl.semaphore_wait(barrier, len(s_peers) + len(q_peers))
    copies[0].start()
    copies[1].start()
    for k in range(1, panels):
        split_inverse(k)
    for k in range(1, panels):
        for j in range(k - 1, -1, -1):
            copies[1 + panels + below.index((k, j))].start()
        copies[1 + k].start()
    for k in range(1, panels):
        k_ref[k] = kernel_rows(panel_points(train_ref, k))

    for k in range(panels - 1):
        for h in range(HALVES):
            for i in range(n_s):
                x_buf[k, h, rows(2 * i + 1 - t), :] = jnp.zeros((unit, mw), jnp.float32)

    for b in range(len(below)):
        keep_block(b, 0, l_ref)

    copies[0].wait_recv()
    other = kernel_rows(panel_points(train_peer, 0))
    for h in range(HALVES):
        r_buf[0, h, block_rows:2 * block_rows, :] = other[:, h * mw:(h + 1) * mw]

    def sem_of(stage, k, h):
        return (stage * panels + k) * HALVES + h

    def send(stage, k, h, src, dst, device):
        number = sem_of(stage, k, h)
        pltpu.make_async_remote_copy(
            src_ref=src, dst_ref=dst, send_sem=send_sem.at[number], recv_sem=recv_sem.at[number],
            device_id=device, device_id_type=MESH,
        ).start()

    s_rows = pl.ds(0, len(s_peers) * unit)
    q_rows = pl.ds(0, len(q_peers) * unit)

    def apply_inverse(k, h):
        if k > 0:
            wait(r_buf.at[k, h, q_rows], recv_sem.at[sem_of(3, k - 1, h)])
        p_buf[k, h] = dot_split(w_high[k], w_low[k], r_buf[k, h])
        for d, device in s_peers:
            send(0, k, h, p_buf.at[k, h, rows((s + d) % n_s)], p_in.at[k, h, rows(d - 1)], device)

    def sum_solved(k, h):
        wait(p_in.at[k, h, s_rows], recv_sem.at[sem_of(0, k, h)])
        total = p_buf[k, h, rows(s), :]
        for d in range(n_s - 1):
            total = total + p_in[k, h, d * unit:(d + 1) * unit, :]
        out_ref[k, :, h * mw:(h + 1) * mw] = total
        if k < panels - 1:
            x_buf[k, h, rows(row), :] = total
            for d, device in s_peers:
                send(1, k, h, x_buf.at[k, h, rows(row)], x_buf.at[k, h, rows(row)], device)

    def apply_factor(k, h):
        wait(x_buf.at[k, h, s_rows], recv_sem.at[sem_of(1, k, h)])
        x = x_buf[k, h]
        b = below.index((k + 1, k))
        change = dot_split(l_high[b], l_low[b], x)
        s_buf[k, h] = change + acc[k + 1, h] if k > 0 else change
        for number, (dt, dc, device) in enumerate(q_peers):
            source = rows(dt * n_col + (col + dc) % n_col)
            send(2, k, h, s_buf.at[k, h, source], s_in.at[k, h, rows(number)], device)

    def add_earlier(k, j, h):
        b = below.index((k + 1, j))
        change = dot_split(l_high[b], l_low[b], x_buf[j, h])
        acc[k + 1, h] = change + acc[k + 1, h] if j > 0 else change

    def sum_residual(k, h):
        wait(s_in.at[k, h, q_rows], recv_sem.at[sem_of(2, k, h)])
        total = s_buf[k, h, rows(col), :]
        for number in range(len(q_peers)):
            total = total + s_in[k, h, number * unit:(number + 1) * unit, :]
        r_buf[k + 1, h, rows(col), :] = k_ref[k + 1, rows(col), h * mw:(h + 1) * mw] - total
        for dt, dc, device in q_peers:
            send(
                3, k, h, r_buf.at[k + 1, h, rows(col)], r_buf.at[k + 1, h, rows(dt * n_col + col)], device
            )

    stages = []
    for k in range(panels):
        stages += [(apply_inverse, k), (sum_solved, k)]
        if k < panels - 1:
            stages += [(apply_factor, k), (sum_residual, k)]
    for tick in range(len(stages) + (HALVES - 1) * LAG):
        for h in range(HALVES):
            at = tick - h * LAG
            if not 0 <= at < len(stages):
                continue
            stage, k = stages[at]
            if h == 0 and stage is apply_inverse:
                take_inverse(k)
            if stage is apply_factor:
                for j in range(k, -1, -1):
                    if h == 0:
                        take_block(below.index((k + 1, j)))
                    if j < k:
                        add_earlier(k, j, h)
            stage(k, h)

    for copy in copies:
        copy.wait_send()
    for k in range(panels):
        for h in range(HALVES):
            wait(p_in.at[k, h, s_rows], send_sem.at[sem_of(0, k, h)])
            if k < panels - 1:
                wait(p_in.at[k, h, s_rows], send_sem.at[sem_of(1, k, h)])
                wait(s_in.at[k, h, q_rows], send_sem.at[sem_of(2, k, h)])
                wait(s_in.at[k, h, q_rows], send_sem.at[sem_of(3, k, h)])


def on_device(train_points, new_points, lengthscales, factor, diag_inverse):
    n_row, n_col = lax.axis_size("row"), lax.axis_size("col")
    panels, _, block_rows = factor.shape[:3]
    width = factor.shape[5]
    dims, new_count = new_points.shape
    unit = block_rows // n_col
    n_s = n_row // 2
    mw = new_count // HALVES
    below = blocks_below(panels)
    train = train_points.reshape(dims * panels, block_rows)
    lower = jnp.stack([factor[k, 0, :, j, 0, :] for k, j in below])
    inverse = diag_inverse.reshape(panels, block_rows, width)
    f32 = jnp.float32
    scratch = [
        pltpu.VMEM((dims * panels, block_rows), f32),
        pltpu.VMEM((len(below), block_rows, width), f32),
        pltpu.VMEM((panels, width // 2, block_rows), f32),
        pltpu.VMEM((panels, width // 2, block_rows), f32),
        pltpu.VMEM((panels, width // 2, 2 * block_rows), jnp.bfloat16),
        pltpu.VMEM((panels, width // 2, 2 * block_rows), jnp.bfloat16),
        pltpu.VMEM((len(below), 2 * block_rows, width), jnp.bfloat16),
        pltpu.VMEM((len(below), 2 * block_rows, width), jnp.bfloat16),
        pltpu.VMEM((panels, block_rows, new_count), f32),
        pltpu.VMEM((panels, HALVES, 2 * block_rows, mw), f32),
        pltpu.VMEM((panels, HALVES, width // 2, mw), f32),
        pltpu.VMEM((panels, HALVES, (n_s - 1) * unit, mw), f32),
        pltpu.VMEM((panels - 1, HALVES, width, mw), f32),
        pltpu.VMEM((panels - 1, HALVES, 2 * block_rows, mw), f32),
        pltpu.VMEM((panels - 1, HALVES, (2 * n_col - 1) * unit, mw), f32),
        pltpu.VMEM((panels, HALVES, 2 * block_rows, mw), f32),
        pltpu.SemaphoreType.DMA((4 * panels * HALVES,)),
        pltpu.SemaphoreType.DMA((4 * panels * HALVES,)),
        pltpu.SemaphoreType.DMA((1 + panels + len(below),)),
        pltpu.SemaphoreType.DMA((1 + panels + len(below),)),
    ]
    solved = pl.pallas_call(
        functools.partial(kernel, n_row, n_col, panels, dims, unit),
        out_shape=jax.ShapeDtypeStruct((panels, unit, new_count), f32),
        in_specs=[pl.BlockSpec(memory_space=pltpu.VMEM)] * 5,
        out_specs=pl.BlockSpec(memory_space=pltpu.VMEM),
        scratch_shapes=scratch,
        compiler_params=pltpu.CompilerParams(
            collective_id=0, has_side_effects=True,
            vmem_limit_bytes=(12 << 20) + 44 * block_rows * width * 4,
        ),
        cost_estimate=pl.CostEstimate(
            flops=12 * block_rows * width * new_count * panels,
            bytes_accessed=8 * panels * block_rows * width * 4,
            transcendentals=panels * block_rows * new_count,
        ),
    )(train, new_points, lengthscales.reshape(1, dims), lower, inverse)
    return solved.reshape(panels, 1, 1, unit, new_count)


def solution(mesh):
    return jax.shard_map(
        on_device,
        mesh=mesh,
        in_specs=(
            P(None, None, "row", None),
            P(),
            P(),
            P(None, "row", None, None, "col", None),
            P(None, "row", None, "col", None),
        ),
        out_specs=P(None, "col", "row", None, None),
        check_vma=False,
    )
```

```python
import functools

import jax
import jax.numpy as jnp
from jax import lax
from jax.experimental import pallas as pl
from jax.experimental.pallas import tpu as pltpu
from jax.sharding import PartitionSpec as P

MESH = pl.DeviceIdType.MESH
HIGHEST = lax.Precision.HIGHEST
HALVES = 1
LAG = 0


def dot(a, b):
    return jnp.dot(a, b, precision=HIGHEST, preferred_element_type=jnp.float32)


def split(a):
    high = a.astype(jnp.bfloat16)
    return high, (a - high.astype(jnp.float32)).astype(jnp.bfloat16)


def dot_split(a_high, a_low, b):
    high, low = split(b)
    wide = jnp.dot(a_high, jnp.concatenate([high, low], axis=1), preferred_element_type=jnp.float32)
    cross = jnp.dot(a_low, high, preferred_element_type=jnp.float32)
    n = b.shape[1]
    return wide[:, :n] + (wide[:, n:] + cross)


def blocks_below(panels):
    return [(k, j) for k in range(panels) for j in range(k)]


def kernel(
    n_row, n_col, panels, dims, unit,
    train_ref, new_ref, lens_ref, l_ref, w_ref, out_ref,
    train_peer, l_peer, w_peer, w_send, w_high, w_low, l_high, l_low, k_ref, r_buf, p_buf, p_in, x_buf, s_buf, s_in, acc,
    send_sem, recv_sem, pre_send, pre_recv,
):
    row, col = lax.axis_index("row"), lax.axis_index("col")
    n_s = n_row // 2
    s, t = row // 2, row % 2
    width = w_ref.shape[2]
    block_rows = w_ref.shape[1]
    mw = r_buf.shape[3]
    below = blocks_below(panels)
    pair = (2 * s + (1 - t), col)
    s_peers = [(d, (2 * ((s + d) % n_s) + t, col)) for d in range(1, n_s)]
    q_offsets = [(dt, dc) for dt in range(2) for dc in range(n_col) if dt + dc > 0]
    q_peers = [
        (dt, dc, (2 * s + (t + dt) % 2, (col + dc) % n_col)) for dt, dc in q_offsets
    ]

    barrier = pltpu.get_barrier_semaphore()
    for device in [p[-1] for p in s_peers] + [p[-1] for p in q_peers]:
        pl.semaphore_signal(barrier, inc=1, device_id=device, device_id_type=MESH)

    def rows(number):
        return pl.ds(pl.multiple_of(number * unit, unit), unit)

    def wait(ref, sem):
        pltpu.make_async_copy(ref, ref, sem).wait()

    def pair_copy(src, dst, number):
        return pltpu.make_async_remote_copy(
            src_ref=src, dst_ref=dst, send_sem=pre_send.at[number], recv_sem=pre_recv.at[number],
            device_id=pair, device_id_type=MESH,
        )

    copies = [pair_copy(train_ref, train_peer, 0)]
    for k in range(panels):
        copies.append(pair_copy(w_send.at[k], w_peer.at[k], 1 + k))
    for b in range(len(below)):
        copies.append(pair_copy(l_ref.at[b], l_peer.at[b], 1 + panels + b))

    def split_inverse(k):
        for b in range(width // 128):
            turned = w_ref[k, :, b * 128:(b + 1) * 128].T
            even = [turned[i * unit:(i + 1) * unit] for i in range(0, 128 // unit, 2)]
            odd = [turned[i * unit:(i + 1) * unit] for i in range(1, 128 // unit, 2)]
            even, odd = jnp.concatenate(even, axis=0), jnp.concatenate(odd, axis=0)
            high, low = split(jnp.where(t == 0, even, odd))
            w_high[k, b * 64:(b + 1) * 64, 0:block_rows] = high
            w_low[k, b * 64:(b + 1) * 64, 0:block_rows] = low
            w_send[k, b * 64:(b + 1) * 64, :] = jnp.where(t == 0, odd, even)

    def keep_block(b, side, ref):
        high, low = split(ref[b])
        l_high[b, side * block_rows:(side + 1) * block_rows, :] = high
        l_low[b, side * block_rows:(side + 1) * block_rows, :] = low

    def take_block(b):
        copies[1 + panels + b].wait_recv()
        keep_block(b, 1, l_peer)

    def take_inverse(k):
        copies[1 + k].wait_recv()
        high, low = split(w_peer[k])
        w_high[k, :, block_rows:2 * block_rows] = high
        w_low[k, :, block_rows:2 * block_rows] = low

    split_inverse(0)
    diagonal = lax.broadcasted_iota(jnp.int32, (dims, dims), 0) == lax.broadcasted_iota(
        jnp.int32, (dims, dims), 1
    )
    lens = jnp.sum(
        jnp.where(diagonal, jnp.broadcast_to(lens_ref[...], (dims, dims)), 0.0), axis=1, keepdims=True
    )
    scaled_new = new_ref[...] / lens
    new_square = jnp.sum(scaled_new * scaled_new, axis=0, keepdims=True)

    def kernel_rows(points):
        turned = (points / lens).T
        square = jnp.sum(turned * turned, axis=1, keepdims=True)
        return jnp.exp(-0.5 * (square + new_square - 2.0 * dot(turned, scaled_new)))

    def panel_points(ref, k):
        return ref[pl.ds(k, dims, stride=panels), :]

    own = kernel_rows(panel_points(train_ref, 0))
    for h in range(HALVES):
        r_buf[0, h, 0:block_rows, :] = own[:, h * mw:(h + 1) * mw]
    pl.semaphore_wait(barrier, len(s_peers) + len(q_peers))
    copies[0].start()
    copies[1].start()
    for k in range(1, panels):
        split_inverse(k)
    for k in range(1, panels):
        for j in range(k - 1, -1, -1):
            copies[1 + panels + below.index((k, j))].start()
        copies[1 + k].start()
    for k in range(1, panels):
        k_ref[k] = kernel_rows(panel_points(train_ref, k))

    for k in range(panels - 1):
        for h in range(HALVES):
            for i in range(n_s):
                x_buf[k, h, rows(2 * i + 1 - t), :] = jnp.zeros((unit, mw), jnp.float32)

    for b in range(len(below)):
        keep_block(b, 0, l_ref)

    copies[0].wait_recv()
    other = kernel_rows(panel_points(train_peer, 0))
    for h in range(HALVES):
        r_buf[0, h, block_rows:2 * block_rows, :] = other[:, h * mw:(h + 1) * mw]

    def sem_of(stage, k, h):
        return (stage * panels + k) * HALVES + h

    def send(stage, k, h, src, dst, device):
        number = sem_of(stage, k, h)
        pltpu.make_async_remote_copy(
            src_ref=src, dst_ref=dst, send_sem=send_sem.at[number], recv_sem=recv_sem.at[number],
            device_id=device, device_id_type=MESH,
        ).start()

    s_rows = pl.ds(0, len(s_peers) * unit)
    q_rows = pl.ds(0, len(q_peers) * unit)

    def apply_inverse(k, h):
        if k > 0:
            wait(r_buf.at[k, h, q_rows], recv_sem.at[sem_of(3, k - 1, h)])
        p_buf[k, h] = dot_split(w_high[k], w_low[k], r_buf[k, h])
        for d, device in s_peers:
            send(0, k, h, p_buf.at[k, h, rows((s + d) % n_s)], p_in.at[k, h, rows(d - 1)], device)

    def sum_solved(k, h):
        wait(p_in.at[k, h, s_rows], recv_sem.at[sem_of(0, k, h)])
        total = p_buf[k, h, rows(s), :]
        for d in range(n_s - 1):
            total = total + p_in[k, h, d * unit:(d + 1) * unit, :]
        out_ref[k, :, h * mw:(h + 1) * mw] = total
        if k < panels - 1:
            x_buf[k, h, rows(row), :] = total
            for d, device in s_peers:
                send(1, k, h, x_buf.at[k, h, rows(row)], x_buf.at[k, h, rows(row)], device)

    def apply_factor(k, h):
        wait(x_buf.at[k, h, s_rows], recv_sem.at[sem_of(1, k, h)])
        x = x_buf[k, h]
        b = below.index((k + 1, k))
        change = dot_split(l_high[b], l_low[b], x)
        s_buf[k, h] = change + acc[k + 1, h] if k > 0 else change
        for number, (dt, dc, device) in enumerate(q_peers):
            source = rows(dt * n_col + (col + dc) % n_col)
            send(2, k, h, s_buf.at[k, h, source], s_in.at[k, h, rows(number)], device)

    def add_earlier(k, j, h):
        b = below.index((k + 1, j))
        change = dot_split(l_high[b], l_low[b], x_buf[j, h])
        acc[k + 1, h] = change + acc[k + 1, h] if j > 0 else change

    def sum_residual(k, h):
        wait(s_in.at[k, h, q_rows], recv_sem.at[sem_of(2, k, h)])
        total = s_buf[k, h, rows(col), :]
        for number in range(len(q_peers)):
            total = total + s_in[k, h, number * unit:(number + 1) * unit, :]
        r_buf[k + 1, h, rows(col), :] = k_ref[k + 1, rows(col), h * mw:(h + 1) * mw] - total
        for dt, dc, device in q_peers:
            send(
                3, k, h, r_buf.at[k + 1, h, rows(col)], r_buf.at[k + 1, h, rows(dt * n_col + col)], device
            )

    stages = []
    for k in range(panels):
        stages += [(apply_inverse, k), (sum_solved, k)]
        if k < panels - 1:
            stages += [(apply_factor, k), (sum_residual, k)]
    for tick in range(len(stages) + (HALVES - 1) * LAG):
        for h in range(HALVES):
            at = tick - h * LAG
            if not 0 <= at < len(stages):
                continue
            stage, k = stages[at]
            if h == 0 and stage is apply_inverse:
                take_inverse(k)
            if stage is apply_factor:
                for j in range(k, -1, -1):
                    if h == 0:
                        take_block(below.index((k + 1, j)))
                    if j < k:
                        add_earlier(k, j, h)
            stage(k, h)

    for copy in copies:
        copy.wait_send()
    for k in range(panels):
        for h in range(HALVES):
            wait(p_in.at[k, h, s_rows], send_sem.at[sem_of(0, k, h)])
            if k < panels - 1:
                wait(p_in.at[k, h, s_rows], send_sem.at[sem_of(1, k, h)])
                wait(s_in.at[k, h, q_rows], send_sem.at[sem_of(2, k, h)])
                wait(s_in.at[k, h, q_rows], send_sem.at[sem_of(3, k, h)])


def on_device(train_points, new_points, lengthscales, factor, diag_inverse):
    n_row, n_col = lax.axis_size("row"), lax.axis_size("col")
    panels, _, block_rows = factor.shape[:3]
    width = factor.shape[5]
    dims, new_count = new_points.shape
    unit = block_rows // n_col
    n_s = n_row // 2
    mw = new_count // HALVES
    below = blocks_below(panels)
    train = train_points.reshape(dims * panels, block_rows)
    lower = jnp.stack([factor[k, 0, :, j, 0, :] for k, j in below])
    inverse = diag_inverse.reshape(panels, block_rows, width)
    f32 = jnp.float32
    scratch = [
        pltpu.VMEM((dims * panels, block_rows), f32),
        pltpu.VMEM((len(below), block_rows, width), f32),
        pltpu.VMEM((panels, width // 2, block_rows), f32),
        pltpu.VMEM((panels, width // 2, block_rows), f32),
        pltpu.VMEM((panels, width // 2, 2 * block_rows), jnp.bfloat16),
        pltpu.VMEM((panels, width // 2, 2 * block_rows), jnp.bfloat16),
        pltpu.VMEM((len(below), 2 * block_rows, width), jnp.bfloat16),
        pltpu.VMEM((len(below), 2 * block_rows, width), jnp.bfloat16),
        pltpu.VMEM((panels, block_rows, new_count), f32),
        pltpu.VMEM((panels, HALVES, 2 * block_rows, mw), f32),
        pltpu.VMEM((panels, HALVES, width // 2, mw), f32),
        pltpu.VMEM((panels, HALVES, (n_s - 1) * unit, mw), f32),
        pltpu.VMEM((panels - 1, HALVES, width, mw), f32),
        pltpu.VMEM((panels - 1, HALVES, 2 * block_rows, mw), f32),
        pltpu.VMEM((panels - 1, HALVES, (2 * n_col - 1) * unit, mw), f32),
        pltpu.VMEM((panels, HALVES, 2 * block_rows, mw), f32),
        pltpu.SemaphoreType.DMA((4 * panels * HALVES,)),
        pltpu.SemaphoreType.DMA((4 * panels * HALVES,)),
        pltpu.SemaphoreType.DMA((1 + panels + len(below),)),
        pltpu.SemaphoreType.DMA((1 + panels + len(below),)),
    ]
    solved = pl.pallas_call(
        functools.partial(kernel, n_row, n_col, panels, dims, unit),
        out_shape=jax.ShapeDtypeStruct((panels, unit, new_count), f32),
        in_specs=[pl.BlockSpec(memory_space=pltpu.VMEM)] * 5,
        out_specs=pl.BlockSpec(memory_space=pltpu.VMEM),
        scratch_shapes=scratch,
        compiler_params=pltpu.CompilerParams(
            collective_id=0, has_side_effects=True,
            vmem_limit_bytes=(12 << 20) + 44 * block_rows * width * 4,
        ),
        cost_estimate=pl.CostEstimate(
            flops=12 * block_rows * width * new_count * panels,
            bytes_accessed=8 * panels * block_rows * width * 4,
            transcendentals=panels * block_rows * new_count,
        ),
    )(train, new_points, lengthscales.reshape(1, dims), lower, inverse)
    return solved.reshape(panels, 1, 1, unit, new_count)


def solution(mesh):
    return jax.shard_map(
        on_device,
        mesh=mesh,
        in_specs=(
            P(None, None, "row", None),
            P(),
            P(),
            P(None, "row", None, None, "col", None),
            P(None, "row", None, "col", None),
        ),
        out_specs=P(None, "col", "row", None, None),
        check_vma=False,
    )
```
